256 devices in a mesh: lag: 16 (over z, x_hi), col: 16 (over y, x_lo, core).
Axes of the slice: x: 4 (x_hi: 2, x_lo: 2; x = x_hi * 2 + x_lo), y: 4, z: 8, core: 2. Of those that a mesh axis runs over, the one named last changes fastest.
Arguments:
- blocks: bfloat16 [16, 512, 8, 128, 128], P('lag', 'col'), may hold values from -0.046875 to 0.046875
- offsets: int32 [16, 512, 8], P('lag', 'col'), may hold values from -24 to 24
- history: bfloat16 [16, 512, 16, 128], P('lag', 'col'), may hold values from -6 to 6
- instant_inverse: float32 [512, 128, 128], P('col'), may hold values from -0.5 to 0.5
- incident: float32 [2, 512, 16, 256], P(None, 'col', 'lag'), may hold values from -6 to 6
- element_map: int32 [512, 256], P('col'), may hold values from 0 to 127
Outputs:
- currents: bfloat16 [2, 512, 16, 128], P(None, 'col', 'lag')
- history_out: bfloat16 [16, 512, 16, 128], P('lag', 'col')
The draws below stay inside these ranges and needn't reach their ends.
All inputs are finite; a program needn't handle non-finite values.
Results may differ from the reference program's by a relative error of at most 0.015.
Values may be sent and summed in bfloat16 or wider, within the bound.
No kernel may reach another device: no remote copies, remote signals or barrier semaphores. Data moves between devices by JAX's collectives and lax.ppermute only.
A program may use at most 64 MiB of HBM per device.

```python
import jax
import jax.numpy as jnp
from jax import lax

NB = 512
BS = 128
P_SIZE = 16
BW = 8
HALF = 24
STEPS = 2
EB = 256
L = 16


def touch_ends(result, own_key, least, largest):
    longest = result.shape.index(max(result.shape))
    spots = []
    for shift in (0, 1):
        where = [jax.random.randint(jax.random.fold_in(own_key, axis), (), 0, length) for axis, length in enumerate(result.shape)]
        where[longest] = (where[longest] + shift) % result.shape[longest]
        spots.append(tuple(where))
    return result.at[spots[0]].set(least).at[spots[1]].set(largest)


def levels(key, dims, cuts, least, largest):
    level, own = 1.0, jax.random.fold_in(key, 6)
    for dim, parts in cuts:
        steps = jnp.exp(jax.random.uniform(jax.random.fold_in(own, dim), (parts,), jnp.float32, least / len(cuts), largest / len(cuts)))
        level = level * jnp.repeat(steps, dims[dim] // parts).reshape([-1 if axis == dim else 1 for axis in range(len(dims))])
    return level


def noise(own_key, dims, deviation, most, shards=(), kind=jnp.bfloat16):
    gain = levels(own_key, dims, shards, -0.22, 0.18) if shards else 1.0
    entries = jax.random.normal(own_key, dims, jnp.float32) * deviation * gain
    return jnp.minimum(jnp.maximum(entries, -most), most).astype(kind)


def setup_inputs(seed: int = 0) -> dict:
    arg_keys = jax.random.split(jax.random.key(seed), 7)
    return {
        "blocks": noise(arg_keys[0], (L, NB, BW, BS, BS), (BS * BW * L) ** -0.5, 0.046875, ((0, 16), (1, 16))),
        "offsets": touch_ends(jax.random.randint(arg_keys[1], (L, NB, BW), 0 - HALF, HALF + 1), jax.random.fold_in(arg_keys[1], 1), 0 - HALF, HALF).astype(jnp.int32),
        "history": noise(arg_keys[2], (L, NB, P_SIZE, BS), 1.0, 6.0, ((0, 16), (1, 16))),
        "instant_inverse": noise(arg_keys[3], (NB, BS, BS), BS ** -0.5, 0.5, ((0, 16),), jnp.float32),
        "incident": noise(arg_keys[4], (STEPS, NB, P_SIZE, EB), 1.0, 6.0, ((1, 16), (2, 16)), jnp.float32),
        "element_map": touch_ends(jax.random.randint(arg_keys[5], (NB, EB), 0, BS), jax.random.fold_in(arg_keys[5], 1), 0, BS - 1).astype(jnp.int32),
    }


def reference(blocks, offsets, history, instant_inverse, incident, element_map):
    columns = jnp.arange(NB, dtype=jnp.int32)
    rows = jnp.clip(columns[None, :, None] + offsets, 0, NB - 1).astype(jnp.int32)
    load = (element_map[:, :, None] == jnp.arange(BS, dtype=jnp.int32)[None, None, :]).astype(jnp.float32)

    def shell_term(total, pieces):
        blk, rws, cur = pieces
        prod = jnp.einsum('ckij,cpj->ckpi', blk.astype(jnp.float32), cur.astype(jnp.float32))
        total = total.at[rws.reshape(-1)].add(prod.reshape(-1, P_SIZE, BS))
        return total, None

    outs = []
    for step in range(STEPS):
        start = jnp.zeros((NB, P_SIZE, BS), jnp.float32)
        partial_value, unused = lax.scan(shell_term, start, (blocks, rows, history))
        source = jnp.einsum('bpe,bei->bpi', incident[step], load, precision=lax.Precision.HIGHEST)
        current = jnp.einsum('bij,bpj->bpi', instant_inverse, source - partial_value, precision=lax.Precision.HIGHEST).astype(jnp.bfloat16)
        outs.append(current)
        history = jnp.concatenate([current[None], history[:-1]], axis=0)
    return jnp.stack(outs), history
```

```python
import functools

import jax
import jax.numpy as jnp
from jax import lax
from jax.experimental import pallas as pl
from jax.experimental.pallas import tpu as pltpu
from jax.sharding import PartitionSpec as P

F32 = jnp.float32
BF16 = jnp.bfloat16
HALF = 24
NT = (((1,), (1,)), ((), ()))
VMEM = pl.BlockSpec(memory_space=pltpu.VMEM)
SMEM = pl.BlockSpec(memory_space=pltpu.SMEM)


def split(x):
    high = x.astype(BF16)
    return high, (x - high.astype(F32)).astype(BF16)


def banded(place_ref, offsets_ref, hist, blocks, window, total_blocks):
    block_cols, width, size, _ = blocks.shape
    first = place_ref[0]
    window[...] = jnp.zeros_like(window)

    def columns(i, carry):
        for j in range(4):
            c = i * 4 + j
            column = blocks[c].reshape(width * size, size)
            prod = lax.dot_general(hist[c], column, NT, preferred_element_type=F32)
            for k in range(width):
                row = jnp.clip(first + c + offsets_ref[k, c], 0, total_blocks - 1) - first + HALF
                window[row] += prod[:, size * k : size * (k + 1)]
        return carry

    lax.fori_loop(0, block_cols // 4, columns, 0)


def hand_out(window, main, up, down):
    n = main.shape[0]
    main[...] = window[HALF : HALF + n]
    up[...] = window[HALF + n :].astype(BF16)
    down[...] = window[:HALF].astype(BF16)


def partial_kernel(total_blocks, place_ref, offsets_ref, hist, blocks, main, up, down, window):
    banded(place_ref, offsets_ref, hist, blocks, window, total_blocks)
    hand_out(window, main, up, down)


def prepare_kernel(incident, element_map, inverse, source, inverse_parts):
    n, size, _ = inverse.shape
    samples = element_map.shape[1]
    unknown = lax.broadcasted_iota(jnp.int32, (size, samples), 0)
    line = lax.broadcasted_iota(jnp.int32, (8, samples), 0)
    for b in range(n):
        load = (unknown == element_map[b : b + 1, :]).astype(F32).astype(BF16)
        rows = jnp.zeros((8, samples), F32)
        for t in range(2):
            sample = jnp.broadcast_to(incident[t, b], (8, samples))
            high = sample.astype(BF16).astype(F32)
            rows = jnp.where(line == 2 * t, high, jnp.where(line == 2 * t + 1, sample - high, rows))
        out = lax.dot_general(rows.astype(BF16), load, NT, preferred_element_type=F32)
        for t in range(2):
            source[t, b : b + 1, :] = out[2 * t : 2 * t + 1] + out[2 * t + 1 : 2 * t + 2]
        high, low = split(inverse[b])
        inverse_parts[b, :, :size] = high
        inverse_parts[b, :, size:] = low


def combine_kernel(place_ref, main, from_below, from_above, source, out):
    n, pulses, size = main.shape
    mine = lax.broadcasted_iota(jnp.int32, (1, pulses, size), 1) == place_ref[1]
    for b in range(n):
        value = main[b]
        if b < HALF:
            value = value + from_below[b].astype(F32)
        if b >= n - HALF:
            value = value + from_above[b - (n - HALF)].astype(F32)
        value = value - jnp.where(mine[0], source[b : b + 1, :], 0.0)
        out[b] = value.astype(BF16)


def solve(rest, inverse_part):
    pulses, size = rest.shape
    high, low = split(-rest)
    lhs = jnp.concatenate(
        [jnp.concatenate([high, high], 1), jnp.concatenate([low, jnp.zeros_like(low)], 1)], 0
    )
    out = lax.dot_general(lhs, inverse_part, NT, preferred_element_type=F32)
    return out[:pulses] + out[pulses:]


def first_step_kernel(
    total_blocks, place_ref, offsets_ref, own, far1, far2, far3, inverse_parts, blocks,
    current, own_pulse, main, up, down, window,
):
    n, pulses, size = own.shape
    mine = lax.broadcasted_iota(jnp.int32, (pulses, size), 0) == place_ref[1]
    for b in range(n):
        rest = sum(part[b].astype(F32) for part in (far1, far2, far3)) + own[b].astype(F32)
        new = solve(rest, inverse_parts[b])
        current[b] = new.astype(BF16)
        own_pulse[b : b + 1, :] = jnp.sum(jnp.where(mine, new, 0.0), axis=0, keepdims=True)
    banded(place_ref, offsets_ref, current, blocks, window, total_blocks)
    hand_out(window, main, up, down)


def second_step_kernel(
    own, far1, far2, far3, main, from_below, from_above, inverse_parts,
    current, by_pulse, scratch,
):
    n, pulses, size = own.shape
    for b in range(n):
        rest = sum(part[b].astype(F32) for part in (far1, far2, far3)) + own[b].astype(F32)
        rest = rest + main[b]
        if b < HALF:
            rest = rest + from_below[b].astype(F32)
        if b >= n - HALF:
            rest = rest + from_above[b - (n - HALF)].astype(F32)
        new = solve(rest, inverse_parts[b])
        current[b] = new.astype(BF16)
        scratch[b * pulses : (b + 1) * pulses, :] = new
    for p in range(pulses):
        by_pulse[p] = scratch[pl.ds(p, n, stride=pulses), :].astype(BF16)


def call(kernel, name, out_shape, in_specs, scratch_shapes=()):
    return pl.pallas_call(
        kernel,
        name=name,
        out_shape=out_shape,
        in_specs=in_specs,
        out_specs=[VMEM] * len(out_shape),
        scratch_shapes=scratch_shapes,
        compiler_params=pltpu.CompilerParams(vmem_limit_bytes=16 * 2**20),
    )


def exchange(block, distance):
    return lax.ppermute(block, "lag", [(i, i ^ distance) for i in range(16)])


def halo(up, down):
    n = lax.axis_size("col")
    from_below = lax.ppermute(up, "col", [(i, i + 1) for i in range(n - 1)])
    from_above = lax.ppermute(down, "col", [(i + 1, i) for i in range(n - 1)])
    return from_below, from_above


def near_sum(block):
    total = block.astype(F32)
    for distance in (1, 2, 3):
        total = total + exchange(block, distance).astype(F32)
    return total.astype(BF16)


def body(blocks, offsets, history, instant_inverse, incident, element_map):
    lag_index = lax.axis_index("lag")
    lags = lax.axis_size("lag")
    n, pulses, size = history.shape[1:]
    width = blocks.shape[2]
    total_blocks = n * lax.axis_size("col")
    place = jnp.stack([lax.axis_index("col") * n, lag_index]).astype(jnp.int32)
    blocks = blocks[0]
    band_rows = offsets[0].T
    shells = history[0]

    def shape(*dims, dtype=F32):
        return jax.ShapeDtypeStruct(dims, dtype)

    window = pltpu.VMEM((n + 2 * HALF, pulses, size), F32)
    partial_out = (
        shape(n, pulses, size),
        shape(HALF, pulses, size, dtype=BF16),
        shape(HALF, pulses, size, dtype=BF16),
    )

    partial = call(
        functools.partial(partial_kernel, total_blocks), "partial",
        partial_out, [SMEM, SMEM, VMEM, VMEM], [window],
    )
    prepare = call(
        prepare_kernel, "prepare",
        (shape(2, n, size), shape(n, size, 2 * size, dtype=BF16)), [VMEM] * 3,
    )
    combine = call(
        combine_kernel, "combine", (shape(n, pulses, size, dtype=BF16),), [SMEM] + [VMEM] * 4,
    )
    first_step = call(
        functools.partial(first_step_kernel, total_blocks), "first_step",
        (shape(n, pulses, size, dtype=BF16), shape(n, size)) + partial_out,
        [SMEM, SMEM] + [VMEM] * 6, [window],
    )
    second_step = call(
        second_step_kernel, "second_step",
        (shape(n, pulses, size, dtype=BF16), shape(pulses, n, size, dtype=BF16)),
        [VMEM] * 8, [pltpu.VMEM((n * pulses, size), F32)],
    )

    with jax.named_scope("shells_step0"):
        main0, up0, down0 = partial(place, band_rows, shells, blocks)
    older = lax.ppermute(shells, "lag", [(i, i + 1) for i in range(lags - 1)])
    oldest = lax.ppermute(shells, "lag", [(i, i + 2) for i in range(lags - 2)])
    with jax.named_scope("halo0"):
        below0, above0 = halo(up0, down0)
    source, inverse_parts = prepare(incident, element_map, instant_inverse)
    (rest0,) = combine(place, main0, below0, above0, source[0])
    with jax.named_scope("near0"):
        near0 = near_sum(rest0)
    with jax.named_scope("shells_step1"):
        main1, up1, down1 = partial(place, band_rows, older, blocks)
    with jax.named_scope("halo1"):
        below1, above1 = halo(up1, down1)
    (rest1,) = combine(place, main1, below1, above1, source[1])
    with jax.named_scope("far0"):
        far0 = [exchange(near0, distance) for distance in (4, 8, 12)]
    with jax.named_scope("near1"):
        near1 = near_sum(rest1)
    with jax.named_scope("far1"):
        far1 = [exchange(near1, distance) for distance in (4, 8, 12)]
    current0, own0, extra, up, down = first_step(
        place, band_rows, near0, *far0, inverse_parts, blocks
    )
    with jax.named_scope("halo_extra"):
        below, above = halo(up, down)
    current1, by_pulse = second_step(near1, *far1, extra, below, above, inverse_parts)
    with jax.named_scope("spread"):
        group = pulses // 4
        parts = [
            lax.ppermute(by_pulse[group * g : group * (g + 1)], "lag", [(0, 4 * g)])
            for g in (1, 2, 3)
        ]
        leader = jnp.where(lag_index == 0, by_pulse[:group], parts[0] + parts[1] + parts[2])
        parts = [
            lax.ppermute(leader[d], "lag", [(4 * g, 4 * g + d) for g in range(4)])
            for d in (1, 2, 3)
        ]
        own1 = jnp.where(lag_index % 4 == 0, leader[0], parts[0] + parts[1] + parts[2])
    currents = jnp.stack([own0.astype(BF16), own1])[:, :, None, :]
    aged = jnp.where(lag_index == 0, current1, jnp.where(lag_index == 1, current0, oldest))
    return currents, aged[None]


def solution(mesh):
    placed = (
        P("lag", "col", None, None, None),
        P("lag", "col", None),
        P("lag", "col", None, None),
        P("col", None, None),
        P(None, "col", "lag", None),
        P("col", None),
    )
    return jax.shard_map(
        body,
        mesh=mesh,
        in_specs=placed,
        out_specs=(P(None, "col", "lag", None), P("lag", "col", None, None)),
        check_vma=False,
    )
```

```python
import functools

import jax
import jax.numpy as jnp
from jax import lax
from jax.experimental import pallas as pl
from jax.experimental.pallas import tpu as pltpu
from jax.sharding import PartitionSpec as P

F32 = jnp.float32
BF16 = jnp.bfloat16
HALF = 24
NT = (((1,), (1,)), ((), ()))
VMEM = pl.BlockSpec(memory_space=pltpu.VMEM)
HBM = pl.BlockSpec(memory_space=pltpu.HBM)
SMEM = pl.BlockSpec(memory_space=pltpu.SMEM)


def split(x):
    high = x.astype(BF16)
    return high, (x - high.astype(F32)).astype(BF16)


def banded(place_ref, offsets_ref, rows_of, blocks, window, total_blocks, chunks, arrived=None):
    block_cols, width, size, _ = blocks.shape
    first = place_ref[0]
    window[...] = jnp.zeros_like(window)

    def columns(i, carry):
        if arrived is not None:
            arrived(i)
        for j in range(block_cols // chunks):
            c = i * (block_cols // chunks) + j
            column = blocks[c].reshape(width * size, size)
            prod = lax.dot_general(rows_of(c), column, NT, preferred_element_type=F32)
            for k in range(width):
                row = jnp.clip(first + c + offsets_ref[k, c], 0, total_blocks - 1) - first + HALF
                window[row] += prod[:, size * k : size * (k + 1)]
        return carry

    lax.fori_loop(0, chunks, columns, 0)


def hand_out(place_ref, windows, main, first_out, second_out):
    n = main.shape[0]
    even = 1 - place_ref[2]
    for t, window in enumerate(windows):
        rows = slice(t * window.shape[1], (t + 1) * window.shape[1])
        main[:, rows] = window[HALF : HALF + n]
        first_out[:, rows] = window[pl.ds(even * (HALF + n), HALF)].astype(BF16)
        second_out[:, rows] = window[pl.ds((1 - even) * (HALF + n), HALF)].astype(BF16)


def take_in(place_ref, main, first_in, second_in):
    n = main.shape[0]
    even = 1 - place_ref[2]
    main[pl.ds(even * (n - HALF), HALF)] += first_in[...].astype(F32)
    main[pl.ds((1 - even) * (n - HALF), HALF)] += second_in[...].astype(F32)


def first_shells_kernel(
    total_blocks, place_ref, offsets_hbm, shells_hbm, blocks_hbm, window, blocks, shells, offsets_ref, sems
):
    chunks = sems.shape[0] - 2
    some = blocks.shape[0] // chunks

    def copy(i):
        part = pl.ds(i * some, some)
        return pltpu.make_async_copy(blocks_hbm.at[part], blocks.at[part], sems.at[i])

    small = [
        pltpu.make_async_copy(offsets_hbm, offsets_ref, sems.at[chunks]),
        pltpu.make_async_copy(shells_hbm, shells, sems.at[chunks + 1]),
    ]
    for each in small:
        each.start()
    for i in range(chunks):
        copy(i).start()
    for each in small:
        each.wait()
    banded(
        place_ref, offsets_ref, lambda c: shells[c], blocks, window, total_blocks, chunks,
        lambda i: copy(i).wait(),
    )


def second_shells_kernel(
    total_blocks, place_ref, offsets_ref, older, first_window, blocks,
    main, first_out, second_out, kept, window,
):
    banded(place_ref, offsets_ref, lambda c: older[c], blocks, window, total_blocks, 2)
    hand_out(place_ref, (first_window, window), main, first_out, second_out)


def prepare_kernel(incident, element_map, inverse, source, inverse_parts):
    n, size, _ = inverse.shape
    samples = element_map.shape[1]
    unknown = lax.broadcasted_iota(jnp.int32, (size, samples), 0)
    line = lax.broadcasted_iota(jnp.int32, (8, samples), 0)
    for b in range(n):
        load = (unknown == element_map[b : b + 1, :]).astype(F32).astype(BF16)
        rows = jnp.zeros((8, samples), F32)
        for t in range(2):
            sample = jnp.broadcast_to(incident[t, b], (8, samples))
            high = sample.astype(BF16).astype(F32)
            rows = jnp.where(line == 2 * t, high, jnp.where(line == 2 * t + 1, sample - high, rows))
        out = lax.dot_general(rows.astype(BF16), load, NT, preferred_element_type=F32)
        for t in range(2):
            source[t, b : b + 1, :] = out[2 * t : 2 * t + 1] + out[2 * t + 1 : 2 * t + 2]
        high, low = split(inverse[b])
        inverse_parts[b, :, :size] = high
        inverse_parts[b, :, size:] = low


def combine_kernel(
    place_ref, main, first_in, second_in, source, keep, send1, send2, send3, total, by_pulse
):
    n, rows, size = main.shape
    pulses = rows // 2
    line = lax.broadcasted_iota(jnp.int32, (rows, size), 0)
    for b in range(n):
        value = main[b]
        for t in range(2):
            mine = line == place_ref[1] + t * pulses
            value = value - jnp.where(mine, source[t, b : b + 1, :], 0.0)
        total[b] = value
    take_in(place_ref, total, first_in, second_in)
    flat = total.reshape(n * rows, size)
    for p in range(pulses):
        for t in range(2):
            by_pulse[p, t] = flat[pl.ds(t * pulses + p, n, stride=rows), :].astype(BF16)
    for distance, out in enumerate((keep, send1, send2, send3)):
        out[...] = by_pulse[pl.ds(quarter_of(place_ref, distance, out.shape[0]), out.shape[0])]


def quarter_of(place_ref, distance, quarter):
    return ((place_ref[1] & 3) ^ distance) * quarter


def by_row(place_ref, parts, t, scratch):
    quarter, _, n, _ = parts[0].shape
    for distance, part in enumerate(parts):
        start = quarter_of(place_ref, distance, quarter)
        for i in range(quarter):
            scratch[pl.ds(pl.multiple_of((start + i) * n, n), n), :] = part[i, t].astype(F32)


def solve(rest, inverse_part):
    pulses, size = rest.shape
    high, low = split(-rest)
    lhs = jnp.concatenate(
        [jnp.concatenate([high, high], 1), jnp.concatenate([low, jnp.zeros_like(low)], 1)], 0
    )
    out = lax.dot_general(lhs, inverse_part, NT, preferred_element_type=F32)
    return out[:pulses] + out[pulses:]


def first_step_kernel(
    total_blocks, place_ref, offsets_ref, rest0, rest1, rest2, rest3, inverse_parts, blocks,
    current, own_pulse, main, first_out, second_out, scratch, window,
):
    n, pulses, size = current.shape
    mine = lax.broadcasted_iota(jnp.int32, (pulses, size), 0) == place_ref[1]
    by_row(place_ref, (rest0, rest1, rest2, rest3), 0, scratch)
    for b in range(n):
        new = solve(scratch[pl.ds(b, pulses, stride=n), :], inverse_parts[b])
        current[b] = new.astype(BF16)
        own_pulse[b : b + 1, :] = jnp.sum(jnp.where(mine, new, 0.0), axis=0, keepdims=True)
    banded(place_ref, offsets_ref, lambda c: current[c], blocks, window, total_blocks, 2)
    hand_out(place_ref, (window,), main, first_out, second_out)


def second_step_kernel(
    place_ref, rest0, rest1, rest2, rest3, main, first_in, second_in, inverse_parts, current0, oldest,
    aged, by_pulse, scratch, total,
):
    n, pulses, size = aged.shape
    total[...] = main[...]
    take_in(place_ref, total, first_in, second_in)
    by_row(place_ref, (rest0, rest1, rest2, rest3), 1, scratch)
    for b in range(n):
        value = scratch[pl.ds(b, pulses, stride=n), :] + total[b]
        new = solve(value, inverse_parts[b])
        aged[b] = new.astype(BF16)
        scratch[pl.ds(b, pulses, stride=n), :] = new
    for p in range(pulses):
        by_pulse[p] = scratch[p * n : (p + 1) * n, :].astype(BF16)

    @pl.when(place_ref[1] == 1)
    def _():
        aged[...] = current0[...]

    @pl.when(place_ref[1] > 1)
    def _():
        aged[...] = oldest[...]


def call(kernel, name, out_shape, in_specs, scratch_shapes=(), mib=16, aliases={}):
    return pl.pallas_call(
        kernel,
        name=name,
        out_shape=out_shape,
        in_specs=in_specs,
        out_specs=[VMEM] * len(out_shape),
        scratch_shapes=scratch_shapes,
        input_output_aliases=aliases,
        compiler_params=pltpu.CompilerParams(vmem_limit_bytes=mib * 2**20),
    )


def exchange(block, distance):
    return lax.ppermute(block, "lag", [(i, i ^ distance) for i in range(16)])


def added(own, others):
    return sum((other.astype(F32) for other in others), own.astype(F32)).astype(BF16)


def trade(first_out, second_out):
    n = lax.axis_size("col")
    pairs = [(i, i ^ 1) for i in range(n)]
    others = [(i, i + 1 if i % 2 else i - 1) for i in range(1, n - 1)]
    return lax.ppermute(first_out, "col", pairs), lax.ppermute(second_out, "col", others)


def body(blocks, offsets, history, instant_inverse, incident, element_map):
    lag_index = lax.axis_index("lag")
    lags = lax.axis_size("lag")
    n, pulses, size = history.shape[1:]
    total_blocks = n * lax.axis_size("col")
    col_index = lax.axis_index("col")
    place = jnp.stack([col_index * n, lag_index, col_index % 2]).astype(jnp.int32)
    blocks = blocks[0]
    band_rows = offsets[0].T
    shells = history[0]

    def shape(*dims, dtype=F32):
        return jax.ShapeDtypeStruct(dims, dtype)

    def partial_out(rows):
        edge = shape(HALF, rows, size, dtype=BF16)
        return shape(n, rows, size), edge, edge

    def window(rows):
        return pltpu.VMEM((n + 2 * HALF, rows, size), F32)

    kept = shape(*blocks.shape, dtype=BF16)
    first_shells = call(
        functools.partial(first_shells_kernel, total_blocks), "first_shells",
        (shape(n + 2 * HALF, pulses, size), kept), [SMEM, HBM, HBM, HBM],
        [
            pltpu.VMEM(shells.shape, BF16), pltpu.SMEM(band_rows.shape, jnp.int32),
            pltpu.SemaphoreType.DMA((6,)),
        ],
        mib=40,
    )
    second_shells = call(
        functools.partial(second_shells_kernel, total_blocks), "second_shells",
        partial_out(2 * pulses) + (kept,), [SMEM, SMEM, VMEM, VMEM, VMEM], [window(pulses)],
        aliases={4: 3},
    )
    prepare = call(
        prepare_kernel, "prepare",
        (shape(2, n, size), shape(n, size, 2 * size, dtype=BF16)), [VMEM] * 3,
    )
    combine = call(
        combine_kernel, "combine", (shape(pulses // 4, 2, n, size, dtype=BF16),) * 4,
        [SMEM] + [VMEM] * 4,
        [pltpu.VMEM((n, 2 * pulses, size), F32), pltpu.VMEM((pulses, 2, n, size), BF16)],
    )
    first_step = call(
        functools.partial(first_step_kernel, total_blocks), "first_step",
        (shape(n, pulses, size, dtype=BF16), shape(n, size)) + partial_out(pulses),
        [SMEM, SMEM] + [VMEM] * 6, [pltpu.VMEM((pulses * n, size), F32), window(pulses)],
    )
    second_step = call(
        second_step_kernel, "second_step",
        (shape(n, pulses, size, dtype=BF16), shape(pulses, n, size, dtype=BF16)),
        [SMEM] + [VMEM] * 10,
        [pltpu.VMEM((n * pulses, size), F32), pltpu.VMEM((n, pulses, size), F32)],
    )

    older = lax.ppermute(shells, "lag", [(i, i + 1) for i in range(lags - 1)])
    with jax.named_scope("shells"):
        window0, blocks = first_shells(place, band_rows, shells, blocks)
        main, first_out, second_out, blocks = second_shells(
            place, band_rows, older, window0, blocks
        )
    with jax.named_scope("halo"):
        first_in, second_in = trade(first_out, second_out)
    source, inverse_parts = prepare(incident, element_map, instant_inverse)
    shells, source = lax.optimization_barrier((shells, source))
    oldest = lax.ppermute(shells, "lag", [(i, (i + 2) % lags) for i in range(lags)])
    first_in, second_in, oldest = lax.optimization_barrier((first_in, second_in, oldest))
    keep, *sent = combine(place, main, first_in, second_in, source)
    with jax.named_scope("near"):
        quarter = added(keep, [exchange(part, d) for d, part in zip((1, 2, 3), sent)])
    with jax.named_scope("far"):
        quarter = added(quarter, [exchange(quarter, d) for d in (4, 8, 12)])
    with jax.named_scope("gather"):
        rest = [quarter] + [exchange(quarter, d) for d in (1, 2, 3)]
    current0, own0, extra, first_out, second_out = first_step(
        place, band_rows, *rest, inverse_parts, blocks
    )
    with jax.named_scope("halo_extra"):
        first_in, second_in = trade(first_out, second_out)
    aged, by_pulse1 = second_step(
        place, *rest, extra, first_in, second_in, inverse_parts, current0, oldest
    )
    with jax.named_scope("spread"):
        group = pulses // 4
        parts = [
            lax.ppermute(by_pulse1[group * g : group * (g + 1)], "lag", [(0, 4 * g)])
            for g in (1, 2, 3)
        ]
        leader = jnp.where(lag_index == 0, by_pulse1[:group], parts[0] + parts[1] + parts[2])
        parts = [
            lax.ppermute(leader[d], "lag", [(4 * g, 4 * g + d) for g in range(4)])
            for d in (1, 2, 3)
        ]
        own1 = jnp.where(lag_index % 4 == 0, leader[0], parts[0] + parts[1] + parts[2])
    currents = jnp.stack([own0.astype(BF16), own1])[:, :, None, :]
    return currents, aged[None]


def solution(mesh):
    placed = (
        P("lag", "col", None, None, None),
        P("lag", "col", None),
        P("lag", "col", None, None),
        P("col", None, None),
        P(None, "col", "lag", None),
        P("col", None),
    )
    return jax.shard_map(
        body,
        mesh=mesh,
        in_specs=placed,
        out_specs=(P(None, "col", "lag", None), P("lag", "col", None, None)),
        check_vma=False,
    )
```

```python
import functools

import jax
import jax.numpy as jnp
from jax import lax
from jax.experimental import pallas as pl
from jax.experimental.pallas import tpu as pltpu
from jax.sharding import PartitionSpec as P

F32 = jnp.float32
BF16 = jnp.bfloat16
HALF = 24
NT = (((1,), (1,)), ((), ()))
VMEM = pl.BlockSpec(memory_space=pltpu.VMEM)
HBM = pl.BlockSpec(memory_space=pltpu.HBM)
SMEM = pl.BlockSpec(memory_space=pltpu.SMEM)


def split(x):
    high = x.astype(BF16)
    return high, (x - high.astype(F32)).astype(BF16)


def banded(place_ref, offsets_ref, rows_of, blocks, window, total_blocks, chunks, arrived=None):
    block_cols, width, size, _ = blocks.shape
    first = place_ref[0]
    window[...] = jnp.zeros_like(window)

    def columns(i, carry):
        if arrived is not None:
            arrived(i)
        for j in range(block_cols // chunks):
            c = i * (block_cols // chunks) + j
            column = blocks[c].reshape(width * size, size)
            prod = lax.dot_general(rows_of(c), column, NT, preferred_element_type=F32)
            for k in range(width):
                row = jnp.clip(first + c + offsets_ref[k, c], 0, total_blocks - 1) - first + HALF
                window[row] += prod[:, size * k : size * (k + 1)]
        return carry

    lax.fori_loop(0, chunks, columns, 0)


def hand_out(place_ref, windows, main, first_out, second_out):
    n = main.shape[0]
    even = 1 - place_ref[2]
    for t, window in enumerate(windows):
        rows = slice(t * window.shape[1], (t + 1) * window.shape[1])
        main[:, rows] = window[HALF : HALF + n]
        first_out[:, rows] = window[pl.ds(even * (HALF + n), HALF)].astype(BF16)
        second_out[:, rows] = window[pl.ds((1 - even) * (HALF + n), HALF)].astype(BF16)


def shared(place_ref, b, n, first_in, second_in):
    odd = place_ref[2] == 1
    value = 0.0
    if b < HALF:
        value = value + jnp.where(odd, first_in[b], second_in[b]).astype(F32)
    if b >= n - HALF:
        edge = b - (n - HALF)
        value = value + jnp.where(odd, second_in[edge], first_in[edge]).astype(F32)
    return value


def first_shells_kernel(
    total_blocks, place_ref, offsets_hbm, shells_hbm, blocks_hbm, window, blocks, shells, offsets_ref, sems
):
    chunks = sems.shape[0] - 2
    some = blocks.shape[0] // chunks

    def copy(i):
        part = pl.ds(i * some, some)
        return pltpu.make_async_copy(blocks_hbm.at[part], blocks.at[part], sems.at[i])

    small = [
        pltpu.make_async_copy(offsets_hbm, offsets_ref, sems.at[chunks]),
        pltpu.make_async_copy(shells_hbm, shells, sems.at[chunks + 1]),
    ]
    for each in small:
        each.start()
    for i in range(chunks):
        copy(i).start()
    for each in small:
        each.wait()
    banded(
        place_ref, offsets_ref, lambda c: shells[c], blocks, window, total_blocks, chunks,
        lambda i: copy(i).wait(),
    )


def second_shells_kernel(
    total_blocks, place_ref, offsets_ref, older, first_window, blocks,
    main, first_out, second_out, kept, window,
):
    @pl.when(place_ref[1] > 0)
    def _():
        banded(place_ref, offsets_ref, lambda c: older[c], blocks, window, total_blocks, 2)

    @pl.when(place_ref[1] == 0)
    def _():
        window[...] = jnp.zeros_like(window)

    hand_out(place_ref, (first_window, window), main, first_out, second_out)


def prepare_kernel(incident, element_map, inverse, source, inverse_parts):
    n, size, _ = inverse.shape
    samples = element_map.shape[1]
    unknown = lax.broadcasted_iota(jnp.int32, (size, samples), 0)
    line = lax.broadcasted_iota(jnp.int32, (8, samples), 0)
    for b in range(n):
        load = (unknown == element_map[b : b + 1, :]).astype(F32).astype(BF16)
        rows = jnp.zeros((8, samples), F32)
        for t in range(2):
            sample = jnp.broadcast_to(incident[t, b], (8, samples))
            high = sample.astype(BF16).astype(F32)
            rows = jnp.where(line == 2 * t, high, jnp.where(line == 2 * t + 1, sample - high, rows))
        out = lax.dot_general(rows.astype(BF16), load, NT, preferred_element_type=F32)
        for t in range(2):
            source[t, b : b + 1, :] = out[2 * t : 2 * t + 1] + out[2 * t + 1 : 2 * t + 2]
        high, low = split(inverse[b])
        inverse_parts[b, :, :size] = high
        inverse_parts[b, :, size:] = low


def combine_kernel(
    place_ref, main, first_in, second_in, source, keep, send1, send2, send3, flat, by_pulse
):
    n, rows, size = main.shape
    pulses = rows // 2
    line = lax.broadcasted_iota(jnp.int32, (rows, size), 0)
    for b in range(n):
        value = main[b] + shared(place_ref, b, n, first_in, second_in)
        for t in range(2):
            mine = line == place_ref[1] + t * pulses
            value = value - jnp.where(mine, source[t, b : b + 1, :], 0.0)
        flat[b * rows : (b + 1) * rows, :] = value
    for p in range(pulses):
        for t in range(2):
            by_pulse[p, t] = flat[pl.ds(t * pulses + p, n, stride=rows), :].astype(BF16)
    for distance, out in enumerate((keep, send1, send2, send3)):
        out[...] = by_pulse[pl.ds(quarter_of(place_ref, distance, out.shape[0]), out.shape[0])]


def quarter_of(place_ref, distance, quarter):
    return ((place_ref[1] & 3) ^ distance) * quarter


def by_row(place_ref, parts, t, scratch):
    quarter, _, n, _ = parts[0].shape
    for distance, part in enumerate(parts):
        start = quarter_of(place_ref, distance, quarter)
        for i in range(quarter):
            scratch[pl.ds(pl.multiple_of((start + i) * n, n), n), :] = part[i, t].astype(F32)


def solve(rest, inverse_part):
    pulses, size = rest.shape
    high, low = split(-rest)
    lhs = jnp.concatenate(
        [jnp.concatenate([high, high], 1), jnp.concatenate([low, jnp.zeros_like(low)], 1)], 0
    )
    out = lax.dot_general(lhs, inverse_part, NT, preferred_element_type=F32)
    return out[:pulses] + out[pulses:]


def first_step_kernel(
    total_blocks, place_ref, offsets_ref, rest0, rest1, rest2, rest3, inverse_parts, blocks,
    current, own_pulse, main, first_out, second_out, scratch, window,
):
    n, pulses, size = current.shape
    mine = lax.broadcasted_iota(jnp.int32, (pulses, size), 0) == place_ref[1]
    by_row(place_ref, (rest0, rest1, rest2, rest3), 0, scratch)
    for b in range(n):
        new = solve(scratch[pl.ds(b, pulses, stride=n), :], inverse_parts[b])
        current[b] = new.astype(BF16)
        own_pulse[b : b + 1, :] = jnp.sum(jnp.where(mine, new, 0.0), axis=0, keepdims=True)

    @pl.when(place_ref[1] == 0)
    def _():
        banded(place_ref, offsets_ref, lambda c: current[c], blocks, window, total_blocks, 2)
        hand_out(place_ref, (window,), main, first_out, second_out)


def second_step_kernel(
    place_ref, rest0, rest1, rest2, rest3, main, first_in, second_in, inverse_parts, current0, oldest,
    aged, by_pulse, scratch,
):
    n, pulses, size = aged.shape

    @pl.when(place_ref[1] == 0)
    def _():
        by_row(place_ref, (rest0, rest1, rest2, rest3), 1, scratch)
        for b in range(n):
            value = scratch[pl.ds(b, pulses, stride=n), :] + main[b]
            value = value + shared(place_ref, b, n, first_in, second_in)
            new = solve(value, inverse_parts[b])
            aged[b] = new.astype(BF16)
            scratch[pl.ds(b, pulses, stride=n), :] = new
        for p in range(pulses):
            by_pulse[p] = scratch[p * n : (p + 1) * n, :].astype(BF16)

    @pl.when(place_ref[1] == 1)
    def _():
        aged[...] = current0[...]

    @pl.when(place_ref[1] > 1)
    def _():
        aged[...] = oldest[...]


def call(kernel, name, out_shape, in_specs, scratch_shapes=(), mib=16, aliases={}):
    return pl.pallas_call(
        kernel,
        name=name,
        out_shape=out_shape,
        in_specs=in_specs,
        out_specs=[VMEM] * len(out_shape),
        scratch_shapes=scratch_shapes,
        input_output_aliases=aliases,
        compiler_params=pltpu.CompilerParams(vmem_limit_bytes=mib * 2**20),
    )


def exchange(block, distance):
    return lax.ppermute(block, "lag", [(i, i ^ distance) for i in range(16)])


def added(own, others):
    return sum((other.astype(F32) for other in others), own.astype(F32)).astype(BF16)


def trade(first_out, second_out):
    n = lax.axis_size("col")
    pairs = [(i, i ^ 1) for i in range(n)]
    others = [(i, (i + 1 if i % 2 else i - 1) % n) for i in range(n)]
    return lax.ppermute(first_out, "col", pairs), lax.ppermute(second_out, "col", others)


def body(blocks, offsets, history, instant_inverse, incident, element_map):
    lag_index = lax.axis_index("lag")
    lags = lax.axis_size("lag")
    n, pulses, size = history.shape[1:]
    total_blocks = n * lax.axis_size("col")
    col_index = lax.axis_index("col")
    place = jnp.stack([col_index * n, lag_index, col_index % 2]).astype(jnp.int32)
    blocks = blocks[0]
    band_rows = offsets[0].T
    shells = history[0]

    def shape(*dims, dtype=F32):
        return jax.ShapeDtypeStruct(dims, dtype)

    def partial_out(rows):
        edge = shape(HALF, rows, size, dtype=BF16)
        return shape(n, rows, size), edge, edge

    def window(rows):
        return pltpu.VMEM((n + 2 * HALF, rows, size), F32)

    kept = shape(*blocks.shape, dtype=BF16)
    first_shells = call(
        functools.partial(first_shells_kernel, total_blocks), "first_shells",
        (shape(n + 2 * HALF, pulses, size), kept), [SMEM, HBM, HBM, HBM],
        [
            pltpu.VMEM(shells.shape, BF16), pltpu.SMEM(band_rows.shape, jnp.int32),
            pltpu.SemaphoreType.DMA((6,)),
        ],
        mib=40,
    )
    second_shells = call(
        functools.partial(second_shells_kernel, total_blocks), "second_shells",
        partial_out(2 * pulses) + (kept,), [SMEM, SMEM, VMEM, VMEM, VMEM], [window(pulses)],
        aliases={4: 3},
    )
    prepare = call(
        prepare_kernel, "prepare",
        (shape(2, n, size), shape(n, size, 2 * size, dtype=BF16)), [VMEM] * 3,
    )
    combine = call(
        combine_kernel, "combine", (shape(pulses // 4, 2, n, size, dtype=BF16),) * 4,
        [SMEM] + [VMEM] * 4,
        [pltpu.VMEM((n * 2 * pulses, size), F32), pltpu.VMEM((pulses, 2, n, size), BF16)],
    )
    first_step = call(
        functools.partial(first_step_kernel, total_blocks), "first_step",
        (shape(n, pulses, size, dtype=BF16), shape(n, size)) + partial_out(pulses),
        [SMEM, SMEM] + [VMEM] * 6, [pltpu.VMEM((pulses * n, size), F32), window(pulses)],
    )
    second_step = call(
        second_step_kernel, "second_step",
        (shape(n, pulses, size, dtype=BF16), shape(pulses, n, size, dtype=BF16)),
        [SMEM] + [VMEM] * 10,
        [pltpu.VMEM((n * pulses, size), F32)],
    )

    older = lax.ppermute(shells, "lag", [(i, (i + 1) % lags) for i in range(lags)])
    with jax.named_scope("shells"):
        window0, blocks = first_shells(place, band_rows, shells, blocks)
        main, first_out, second_out, blocks = second_shells(
            place, band_rows, older, window0, blocks
        )
    with jax.named_scope("halo"):
        first_in, second_in = trade(first_out, second_out)
    source, inverse_parts = prepare(incident, element_map, instant_inverse)
    keep, *sent = combine(place, main, first_in, second_in, source)
    with jax.named_scope("near"):
        quarter = added(keep, [exchange(part, d) for d, part in zip((1, 2, 3), sent)])
    with jax.named_scope("far"):
        quarter = added(quarter, [exchange(quarter, d) for d in (4, 8, 12)])
    with jax.named_scope("gather"):
        rest = [quarter] + [exchange(quarter, d) for d in (1, 2, 3)]
    current0, own0, extra, first_out, second_out = first_step(
        place, band_rows, *rest, inverse_parts, blocks
    )
    shells, current0 = lax.optimization_barrier((shells, current0))
    oldest = lax.ppermute(shells, "lag", [(i, (i + 2) % lags) for i in range(lags)])
    with jax.named_scope("halo_extra"):
        first_in, second_in = trade(first_out, second_out)
    aged, by_pulse1 = second_step(
        place, *rest, extra, first_in, second_in, inverse_parts, current0, oldest
    )
    with jax.named_scope("spread"):
        group = pulses // 4
        leader = by_pulse1[:group]
        for g in (1, 2, 3):
            part = lax.ppermute(by_pulse1[group * g : group * (g + 1)], "lag", [(0, 4 * g)])
            leader = jnp.where(lag_index == 4 * g, part, leader)
        own1 = leader[0]
        for d in (1, 2, 3):
            part = lax.ppermute(leader[d], "lag", [(4 * g, 4 * g + d) for g in range(4)])
            own1 = jnp.where(lag_index % 4 == d, part, own1)
    currents = jnp.stack([own0.astype(BF16), own1])[:, :, None, :]
    return currents, aged[None]


def solution(mesh):
    placed = (
        P("lag", "col", None, None, None),
        P("lag", "col", None),
        P("lag", "col", None, None),
        P("col", None, None),
        P(None, "col", "lag", None),
        P("col", None),
    )
    return jax.shard_map(
        body,
        mesh=mesh,
        in_specs=placed,
        out_specs=(P(None, "col", "lag", None), P("lag", "col", None, None)),
        check_vma=False,
    )
```

```python
import functools

import jax
import jax.numpy as jnp
from jax import lax
from jax.experimental import pallas as pl
from jax.experimental.pallas import tpu as pltpu
from jax.sharding import PartitionSpec as P

F32 = jnp.float32
BF16 = jnp.bfloat16
HALF = 24
NT = (((1,), (1,)), ((), ()))
VMEM = pl.BlockSpec(memory_space=pltpu.VMEM)
HBM = pl.BlockSpec(memory_space=pltpu.HBM)
SMEM = pl.BlockSpec(memory_space=pltpu.SMEM)


def split(x):
    high = x.astype(BF16)
    return high, (x - high.astype(F32)).astype(BF16)


def banded(place_ref, offsets_ref, rows_of, blocks, window, total_blocks):
    block_cols, width, size, _ = blocks.shape
    first = place_ref[0]
    window[...] = jnp.zeros_like(window)
    for c in range(block_cols):
        column = blocks[c].reshape(width * size, size)
        prod = lax.dot_general(rows_of(c), column, NT, preferred_element_type=F32)
        for k in range(width):
            row = jnp.clip(first + c + offsets_ref[k, c], 0, total_blocks - 1) - first + HALF
            window[row] += prod[:, size * k : size * (k + 1)]


def hand_out(place_ref, window, main, first_out, second_out):
    n = main.shape[0]
    main[...] = window[HALF : HALF + n]
    even = 1 - place_ref[2]
    first_out[...] = window[pl.ds(even * (HALF + n), HALF)].astype(BF16)
    second_out[...] = window[pl.ds((1 - even) * (HALF + n), HALF)].astype(BF16)


def shared(place_ref, b, n, first_in, second_in):
    odd = place_ref[2] == 1
    value = 0.0
    if b < HALF:
        value = value + jnp.where(odd, first_in[b], second_in[b]).astype(F32)
    if b >= n - HALF:
        edge = b - (n - HALF)
        value = value + jnp.where(odd, second_in[edge], first_in[edge]).astype(F32)
    return value


def fetch_kernel(place_ref, blocks_hbm, blocks, follows, sems):
    chunks = sems.shape[0]
    some = blocks.shape[0] // chunks
    copies = []
    for i in range(chunks):
        part = pl.ds(i * some, some)
        copies.append(pltpu.make_async_copy(blocks_hbm.at[part], blocks.at[part], sems.at[i]))
    for copy in copies:
        copy.start()
    follows[...] = jnp.where(place_ref[1] > 0, jnp.ones_like(follows), jnp.zeros_like(follows))
    for copy in copies:
        copy.wait()


def shells_kernel(
    total_blocks, place_ref, offsets_ref, shells, older, blocks, follows,
    main, first_out, second_out, kept, window,
):
    banded(
        place_ref, offsets_ref, lambda c: jnp.concatenate([shells[c], older[c] * follows[...]], 0),
        blocks, window, total_blocks,
    )
    hand_out(place_ref, window, main, first_out, second_out)


def prepare_kernel(incident, element_map, inverse, source, inverse_parts):
    n, size, _ = inverse.shape
    samples = element_map.shape[1]
    unknown = lax.broadcasted_iota(jnp.int32, (size, samples), 0)
    line = lax.broadcasted_iota(jnp.int32, (8, samples), 0)
    for b in range(n):
        load = (unknown == element_map[b : b + 1, :]).astype(F32).astype(BF16)
        rows = jnp.zeros((8, samples), F32)
        for t in range(2):
            sample = jnp.broadcast_to(incident[t, b], (8, samples))
            high = sample.astype(BF16).astype(F32)
            rows = jnp.where(line == 2 * t, high, jnp.where(line == 2 * t + 1, sample - high, rows))
        out = lax.dot_general(rows.astype(BF16), load, NT, preferred_element_type=F32)
        for t in range(2):
            source[t, b : b + 1, :] = out[2 * t : 2 * t + 1] + out[2 * t + 1 : 2 * t + 2]
        high, low = split(inverse[b])
        inverse_parts[b, :, :size] = high
        inverse_parts[b, :, size:] = low


def combine_kernel(
    place_ref, main, first_in, second_in, source, keep, send1, send2, send3, total
):
    n, both, size = main.shape
    line = lax.broadcasted_iota(jnp.int32, (both, size), 0)
    for b in range(n):
        value = main[b] + shared(place_ref, b, n, first_in, second_in)
        for t in range(2):
            mine = line == place_ref[1] + t * (both // 2)
            value = value - jnp.where(mine, source[t, b : b + 1, :], 0.0)
        total[b] = value.astype(BF16)
    for distance, out in enumerate((keep, send1, send2, send3)):
        out[...] = total[quarter_of(place_ref, distance, n)]


def quarter_of(place_ref, distance, n):
    return pl.ds(((place_ref[1] & 3) ^ distance) * (n // 4), n // 4)


def gathered(place_ref, parts, rest):
    for distance, part in enumerate(parts):
        rest[quarter_of(place_ref, distance, rest.shape[0])] = part[...]


def solve(rest, inverse_part):
    pulses, size = rest.shape
    high, low = split(-rest)
    lhs = jnp.concatenate(
        [jnp.concatenate([high, high], 1), jnp.concatenate([low, jnp.zeros_like(low)], 1)], 0
    )
    out = lax.dot_general(lhs, inverse_part, NT, preferred_element_type=F32)
    return out[:pulses] + out[pulses:]


def first_step_kernel(
    total_blocks, place_ref, offsets_ref, rest0, rest1, rest2, rest3, inverse_parts, blocks,
    current, main, first_out, second_out, rest, window,
):
    n, pulses, size = current.shape
    gathered(place_ref, (rest0, rest1, rest2, rest3), rest)
    for b in range(n):
        current[b] = solve(rest[b, :pulses].astype(F32), inverse_parts[b]).astype(BF16)

    @pl.when(place_ref[1] == 0)
    def _():
        banded(place_ref, offsets_ref, lambda c: current[c], blocks, window, total_blocks)
        hand_out(place_ref, window, main, first_out, second_out)


def second_sum_kernel(
    place_ref, rest0, rest1, rest2, rest3, main, current0, total, own_pulse, rest
):
    n, pulses, size = main.shape
    mine = lax.broadcasted_iota(jnp.int32, (pulses, size), 0) == place_ref[1]
    gathered(place_ref, (rest0, rest1, rest2, rest3), rest)
    for b in range(n):
        total[b] = rest[b, pulses:].astype(F32) + main[b]
        own = jnp.where(mine, current0[b].astype(F32), 0.0)
        own_pulse[b : b + 1, :] = jnp.sum(own, axis=0, keepdims=True)


def second_step_kernel(
    place_ref, total, first_in, second_in, inverse_parts, current, by_pulse, scratch
):
    n, pulses, size = current.shape

    @pl.when(place_ref[1] == 0)
    def _():
        for b in range(n):
            value = total[b] + shared(place_ref, b, n, first_in, second_in)
            new = solve(value, inverse_parts[b])
            current[b] = new.astype(BF16)
            scratch[b * pulses : (b + 1) * pulses, :] = new
        for p in range(pulses):
            by_pulse[p] = scratch[pl.ds(p, n, stride=pulses), :].astype(BF16)


def call(kernel, name, out_shape, in_specs, scratch_shapes=(), mib=16, aliases={}):
    return pl.pallas_call(
        kernel,
        name=name,
        out_shape=out_shape,
        in_specs=in_specs,
        out_specs=[VMEM] * len(out_shape),
        scratch_shapes=scratch_shapes,
        input_output_aliases=aliases,
        compiler_params=pltpu.CompilerParams(vmem_limit_bytes=mib * 2**20),
    )


def exchange(block, distance):
    return lax.ppermute(block, "lag", [(i, i ^ distance) for i in range(16)])


def added(own, others):
    return sum((other.astype(F32) for other in others), own.astype(F32)).astype(BF16)


def trade(first_out, second_out):
    n = lax.axis_size("col")
    pairs = [(i, i ^ 1) for i in range(n)]
    others = [(i, (i + 1 if i % 2 else i - 1) % n) for i in range(n)]
    return lax.ppermute(first_out, "col", pairs), lax.ppermute(second_out, "col", others)


def body(blocks, offsets, history, instant_inverse, incident, element_map):
    lag_index = lax.axis_index("lag")
    lags = lax.axis_size("lag")
    n, pulses, size = history.shape[1:]
    total_blocks = n * lax.axis_size("col")
    col_index = lax.axis_index("col")
    place = jnp.stack([col_index * n, lag_index, col_index % 2]).astype(jnp.int32)
    blocks = blocks[0]
    band_rows = offsets[0].T
    shells = history[0]

    def shape(*dims, dtype=F32):
        return jax.ShapeDtypeStruct(dims, dtype)

    def partial_out(rows):
        edge = shape(HALF, rows, size, dtype=BF16)
        return shape(n, rows, size), edge, edge

    def window(rows):
        return pltpu.VMEM((n + 2 * HALF, rows, size), F32)

    kept = shape(*blocks.shape, dtype=BF16)
    fetch = call(
        fetch_kernel, "fetch", (kept, shape(pulses, size, dtype=BF16)), [SMEM, HBM], [pltpu.SemaphoreType.DMA((8,))], mib=40
    )
    shell_sums = call(
        functools.partial(shells_kernel, total_blocks), "shell_sums",
        partial_out(2 * pulses) + (kept,), [SMEM, SMEM] + [VMEM] * 4, [window(2 * pulses)],
        aliases={4: 3},
    )
    prepare = call(
        prepare_kernel, "prepare",
        (shape(2, n, size), shape(n, size, 2 * size, dtype=BF16)), [VMEM] * 3,
    )
    quarters = (shape(n // 4, 2 * pulses, size, dtype=BF16),) * 4
    rows = pltpu.VMEM((n, 2 * pulses, size), BF16)
    combine = call(combine_kernel, "combine", quarters, [SMEM] + [VMEM] * 4, [rows])
    first_step = call(
        functools.partial(first_step_kernel, total_blocks), "first_step",
        (shape(n, pulses, size, dtype=BF16),) + partial_out(pulses),
        [SMEM, SMEM] + [VMEM] * 6, [rows, window(pulses)],
    )
    second_sum = call(
        second_sum_kernel, "second_sum",
        (shape(n, pulses, size), shape(n, size)), [SMEM] + [VMEM] * 6, [rows],
    )
    second_step = call(
        second_step_kernel, "second_step",
        (shape(n, pulses, size, dtype=BF16), shape(pulses, n, size, dtype=BF16)),
        [SMEM] + [VMEM] * 4, [pltpu.VMEM((n * pulses, size), F32)],
    )

    older = lax.ppermute(shells, "lag", [(i, (i + 1) % lags) for i in range(lags)])
    with jax.named_scope("shells"):
        blocks, follows = fetch(place, blocks)
        main, first_out, second_out, blocks = shell_sums(
            place, band_rows, shells, older, blocks, follows
        )
    with jax.named_scope("halo"):
        first_in, second_in = trade(first_out, second_out)
    source, inverse_parts = prepare(incident, element_map, instant_inverse)
    keep, *sent = combine(place, main, first_in, second_in, source)
    with jax.named_scope("near"):
        quarter = added(keep, [exchange(part, d) for d, part in zip((1, 2, 3), sent)])
    with jax.named_scope("far"):
        quarter = added(quarter, [exchange(quarter, d) for d in (8, 4, 12)])
    with jax.named_scope("gather"):
        rest = [quarter] + [exchange(quarter, d) for d in (1, 2, 3)]
    current0, extra, first_out, second_out = first_step(
        place, band_rows, *rest, inverse_parts, blocks
    )
    shells, current0 = lax.optimization_barrier((shells, current0))
    oldest = lax.ppermute(shells, "lag", [(i, (i + 2) % lags) for i in range(lags)])
    with jax.named_scope("halo_extra"):
        first_in, second_in = trade(first_out, second_out)
    total, own0 = second_sum(place, *rest, extra, current0)
    current1, by_pulse1 = second_step(place, total, first_in, second_in, inverse_parts)
    with jax.named_scope("spread"):
        quarter = pulses // 4
        groups = [by_pulse1[quarter * g : quarter * (g + 1)] for g in range(4)]
        arrived = [lax.ppermute(groups[g], "lag", [(0, 4 * g)]) for g in (1, 2, 3)]
        leader = groups[0]
        for g in (1, 2, 3):
            leader = jnp.where(lag_index == 4 * g, arrived[g - 1], leader)
        arrived = [
            lax.ppermute(leader[d], "lag", [(4 * g, 4 * g + d) for g in range(4)]) for d in (1, 2, 3)
        ]
        own1 = leader[0]
        for d in (1, 2, 3):
            own1 = jnp.where(lag_index % 4 == d, arrived[d - 1], own1)
    currents = jnp.stack([own0.astype(BF16), own1])[:, :, None, :]
    aged = jnp.where(lag_index == 0, current1, jnp.where(lag_index == 1, current0, oldest))
    return currents, aged[None]


def solution(mesh):
    placed = (
        P("lag", "col", None, None, None),
        P("lag", "col", None),
        P("lag", "col", None, None),
        P("col", None, None),
        P(None, "col", "lag", None),
        P("col", None),
    )
    return jax.shard_map(
        body,
        mesh=mesh,
        in_specs=placed,
        out_specs=(P(None, "col", "lag", None), P("lag", "col", None, None)),
        check_vma=False,
    )
```

```python
import functools

import jax
import jax.numpy as jnp
from jax import lax
from jax.experimental import pallas as pl
from jax.experimental.pallas import tpu as pltpu
from jax.sharding import PartitionSpec as P

F32 = jnp.float32
BF16 = jnp.bfloat16
HALF = 24
NT = (((1,), (1,)), ((), ()))
VMEM = pl.BlockSpec(memory_space=pltpu.VMEM)
HBM = pl.BlockSpec(memory_space=pltpu.HBM)
SMEM = pl.BlockSpec(memory_space=pltpu.SMEM)


def split(x):
    high = x.astype(BF16)
    return high, (x - high.astype(F32)).astype(BF16)


def banded(place_ref, offsets_ref, rows_of, blocks, window, total_blocks):
    block_cols, width, size, _ = blocks.shape
    first = place_ref[0]
    window[...] = jnp.zeros_like(window)
    for c in range(block_cols):
        column = blocks[c].reshape(width * size, size)
        prod = lax.dot_general(rows_of(c), column, NT, preferred_element_type=F32)
        for k in range(width):
            row = jnp.clip(first + c + offsets_ref[k, c], 0, total_blocks - 1) - first + HALF
            window[row] += prod[:, size * k : size * (k + 1)]


def hand_out(place_ref, window, main, first_out, second_out):
    n = main.shape[0]
    main[...] = window[HALF : HALF + n]
    even = 1 - place_ref[2]
    first_out[...] = window[pl.ds(even * (HALF + n), HALF)].astype(BF16)
    second_out[...] = window[pl.ds((1 - even) * (HALF + n), HALF)].astype(BF16)


def shared(place_ref, b, n, first_in, second_in):
    odd = place_ref[2] == 1
    value = 0.0
    if b < HALF:
        value = value + jnp.where(odd, first_in[b], second_in[b]).astype(F32)
    if b >= n - HALF:
        edge = b - (n - HALF)
        value = value + jnp.where(odd, second_in[edge], first_in[edge]).astype(F32)
    return value


def fetch_kernel(place_ref, blocks_hbm, blocks, follows, sems):
    chunks = sems.shape[0]
    some = blocks.shape[0] // chunks
    copies = []
    for i in range(chunks):
        part = pl.ds(i * some, some)
        copies.append(pltpu.make_async_copy(blocks_hbm.at[part], blocks.at[part], sems.at[i]))
    for copy in copies:
        copy.start()
    follows[...] = jnp.where(place_ref[1] > 0, jnp.ones_like(follows), jnp.zeros_like(follows))
    for copy in copies:
        copy.wait()


def shells_kernel(
    total_blocks, place_ref, offsets_ref, shells, older, blocks, follows,
    main, first_out, second_out, kept, window,
):
    banded(
        place_ref, offsets_ref, lambda c: jnp.concatenate([shells[c], older[c] * follows[...]], 0),
        blocks, window, total_blocks,
    )
    hand_out(place_ref, window, main, first_out, second_out)


def prepare_kernel(incident, element_map, inverse, source, inverse_parts):
    n, size, _ = inverse.shape
    samples = element_map.shape[1]
    unknown = lax.broadcasted_iota(jnp.int32, (size, samples), 0)
    line = lax.broadcasted_iota(jnp.int32, (8, samples), 0)
    for b in range(n):
        load = (unknown == element_map[b : b + 1, :]).astype(F32).astype(BF16)
        rows = jnp.zeros((8, samples), F32)
        for t in range(2):
            sample = jnp.broadcast_to(incident[t, b], (8, samples))
            high = sample.astype(BF16).astype(F32)
            rows = jnp.where(line == 2 * t, high, jnp.where(line == 2 * t + 1, sample - high, rows))
        out = lax.dot_general(rows.astype(BF16), load, NT, preferred_element_type=F32)
        for t in range(2):
            source[t, b : b + 1, :] = out[2 * t : 2 * t + 1] + out[2 * t + 1 : 2 * t + 2]
        high, low = split(inverse[b])
        inverse_parts[b, :, :size] = high
        inverse_parts[b, :, size:] = low


def combine_kernel(
    place_ref, main, first_in, second_in, source, keep, send1, send2, send3, total
):
    n, both, size = main.shape
    line = lax.broadcasted_iota(jnp.int32, (both, size), 0)
    for b in range(n):
        value = main[b] + shared(place_ref, b, n, first_in, second_in)
        for t in range(2):
            mine = line == place_ref[1] + t * (both // 2)
            value = value - jnp.where(mine, source[t, b : b + 1, :], 0.0)
        total[b] = value.astype(BF16)
    for distance, out in enumerate((keep, send1, send2, send3)):
        out[...] = total[quarter_of(place_ref, distance, n)]


def quarter_of(place_ref, distance, n):
    return pl.ds(((place_ref[1] & 3) ^ distance) * (n // 4), n // 4)


def gathered(place_ref, parts, rest):
    for distance, part in enumerate(parts):
        rest[quarter_of(place_ref, distance, rest.shape[0])] = part[...]


def solve(rest, inverse_part):
    pulses, size = rest.shape
    high, low = split(-rest)
    lhs = jnp.concatenate(
        [jnp.concatenate([high, high], 1), jnp.concatenate([low, jnp.zeros_like(low)], 1)], 0
    )
    out = lax.dot_general(lhs, inverse_part, NT, preferred_element_type=F32)
    return out[:pulses] + out[pulses:]


def first_step_kernel(
    total_blocks, place_ref, offsets_ref, rest0, rest1, rest2, rest3, inverse_parts, blocks,
    current, main, first_out, second_out, rest, window,
):
    n, pulses, size = current.shape
    gathered(place_ref, (rest0, rest1, rest2, rest3), rest)
    for b in range(n):
        current[b] = solve(rest[b, :pulses].astype(F32), inverse_parts[b]).astype(BF16)

    @pl.when(place_ref[1] == 0)
    def _():
        banded(place_ref, offsets_ref, lambda c: current[c], blocks, window, total_blocks)
        hand_out(place_ref, window, main, first_out, second_out)


def second_sum_kernel(
    place_ref, rest0, rest1, rest2, rest3, main, current0, total, own_pulse, rest
):
    n, pulses, size = main.shape
    mine = lax.broadcasted_iota(jnp.int32, (pulses, size), 0) == place_ref[1]
    gathered(place_ref, (rest0, rest1, rest2, rest3), rest)
    for b in range(n):
        total[b] = rest[b, pulses:].astype(F32) + main[b]
        own = jnp.where(mine, current0[b].astype(F32), 0.0)
        own_pulse[b : b + 1, :] = jnp.sum(own, axis=0, keepdims=True)


def second_step_kernel(
    place_ref, total, first_in, second_in, inverse_parts, current, by_pulse, scratch
):
    n, pulses, size = current.shape

    @pl.when(place_ref[1] == 0)
    def _():
        for b in range(n):
            value = total[b] + shared(place_ref, b, n, first_in, second_in)
            new = solve(value, inverse_parts[b])
            current[b] = new.astype(BF16)
            scratch[b * pulses : (b + 1) * pulses, :] = new
        for p in range(pulses):
            by_pulse[p] = scratch[pl.ds(p, n, stride=pulses), :].astype(BF16)


def call(kernel, name, out_shape, in_specs, scratch_shapes=(), mib=16, aliases={}):
    return pl.pallas_call(
        kernel,
        name=name,
        out_shape=out_shape,
        in_specs=in_specs,
        out_specs=[VMEM] * len(out_shape),
        scratch_shapes=scratch_shapes,
        input_output_aliases=aliases,
        compiler_params=pltpu.CompilerParams(vmem_limit_bytes=mib * 2**20),
    )


def exchange(block, distance):
    return lax.ppermute(block, "lag", [(i, i ^ distance) for i in range(16)])


def added(own, others):
    return sum((other.astype(F32) for other in others), own.astype(F32)).astype(BF16)


def trade(first_out, second_out):
    n = lax.axis_size("col")
    pairs = [(i, i ^ 1) for i in range(n)]
    others = [(i, (i + 1 if i % 2 else i - 1) % n) for i in range(n)]
    second_in = lax.ppermute(second_out, "col", others)
    return lax.ppermute(first_out, "col", pairs), second_in


def body(blocks, offsets, history, instant_inverse, incident, element_map):
    lag_index = lax.axis_index("lag")
    lags = lax.axis_size("lag")
    n, pulses, size = history.shape[1:]
    total_blocks = n * lax.axis_size("col")
    col_index = lax.axis_index("col")
    place = jnp.stack([col_index * n, lag_index, col_index % 2]).astype(jnp.int32)
    blocks = blocks[0]
    band_rows = offsets[0].T
    shells = history[0]

    def shape(*dims, dtype=F32):
        return jax.ShapeDtypeStruct(dims, dtype)

    def partial_out(rows):
        edge = shape(HALF, rows, size, dtype=BF16)
        return shape(n, rows, size), edge, edge

    def window(rows):
        return pltpu.VMEM((n + 2 * HALF, rows, size), F32)

    kept = shape(*blocks.shape, dtype=BF16)
    fetch = call(
        fetch_kernel, "fetch", (kept, shape(pulses, size, dtype=BF16)), [SMEM, HBM], [pltpu.SemaphoreType.DMA((8,))], mib=40
    )
    shell_sums = call(
        functools.partial(shells_kernel, total_blocks), "shell_sums",
        partial_out(2 * pulses) + (kept,), [SMEM, SMEM] + [VMEM] * 4, [window(2 * pulses)],
        aliases={4: 3},
    )
    prepare = call(
        prepare_kernel, "prepare",
        (shape(2, n, size), shape(n, size, 2 * size, dtype=BF16)), [VMEM] * 3,
    )
    quarters = (shape(n // 4, 2 * pulses, size, dtype=BF16),) * 4
    rows = pltpu.VMEM((n, 2 * pulses, size), BF16)
    combine = call(combine_kernel, "combine", quarters, [SMEM] + [VMEM] * 4, [rows])
    first_step = call(
        functools.partial(first_step_kernel, total_blocks), "first_step",
        (shape(n, pulses, size, dtype=BF16),) + partial_out(pulses),
        [SMEM, SMEM] + [VMEM] * 6, [rows, window(pulses)],
    )
    second_sum = call(
        second_sum_kernel, "second_sum",
        (shape(n, pulses, size), shape(n, size)), [SMEM] + [VMEM] * 6, [rows],
    )
    second_step = call(
        second_step_kernel, "second_step",
        (shape(n, pulses, size, dtype=BF16), shape(pulses, n, size, dtype=BF16)),
        [SMEM] + [VMEM] * 4, [pltpu.VMEM((n * pulses, size), F32)],
    )

    older = lax.ppermute(shells, "lag", [(i, (i + 1) % lags) for i in range(lags)])
    with jax.named_scope("shells"):
        blocks, follows = fetch(place, blocks)
        main, first_out, second_out, blocks = shell_sums(
            place, band_rows, shells, older, blocks, follows
        )
    with jax.named_scope("halo"):
        first_in, second_in = trade(first_out, second_out)
    source, inverse_parts = prepare(incident, element_map, instant_inverse)
    keep, *sent = combine(place, main, first_in, second_in, source)
    with jax.named_scope("near"):
        quarter = added(keep, [exchange(sent[d - 1], d) for d in (3, 1, 2)])
    with jax.named_scope("far"):
        quarter = added(quarter, [exchange(quarter, d) for d in (8, 4, 12)])
    with jax.named_scope("gather"):
        by_distance = {d: exchange(quarter, d) for d in (3, 1, 2)}
        rest = [quarter] + [by_distance[d] for d in (1, 2, 3)]
    current0, extra, first_out, second_out = first_step(
        place, band_rows, *rest, inverse_parts, blocks
    )
    shells, current0 = lax.optimization_barrier((shells, current0))
    oldest = lax.ppermute(shells, "lag", [(i, (i + 2) % lags) for i in range(lags)])
    with jax.named_scope("halo_extra"):
        first_in, second_in = trade(first_out, second_out)
    total, own0 = second_sum(place, *rest, extra, current0)
    current1, by_pulse1 = second_step(place, total, first_in, second_in, inverse_parts)
    with jax.named_scope("spread"):
        quarter = pulses // 4
        groups = [by_pulse1[quarter * g : quarter * (g + 1)] for g in range(4)]
        arrived = [lax.ppermute(groups[g], "lag", [(0, 4 * g)]) for g in (1, 2, 3)]
        leader = groups[0]
        for g in (1, 2, 3):
            leader = jnp.where(lag_index == 4 * g, arrived[g - 1], leader)
        arrived = [
            lax.ppermute(leader[d], "lag", [(4 * g, 4 * g + d) for g in range(4)]) for d in (1, 2, 3)
        ]
        own1 = leader[0]
        for d in (1, 2, 3):
            own1 = jnp.where(lag_index % 4 == d, arrived[d - 1], own1)
    currents = jnp.stack([own0.astype(BF16), own1])[:, :, None, :]
    aged = jnp.where(lag_index == 0, current1, jnp.where(lag_index == 1, current0, oldest))
    return currents, aged[None]


def solution(mesh):
    placed = (
        P("lag", "col", None, None, None),
        P("lag", "col", None),
        P("lag", "col", None, None),
        P("col", None, None),
        P(None, "col", "lag", None),
        P("col", None),
    )
    return jax.shard_map(
        body,
        mesh=mesh,
        in_specs=placed,
        out_specs=(P(None, "col", "lag", None), P("lag", "col", None, None)),
        check_vma=False,
    )
```

```python
import functools

import jax
import jax.numpy as jnp
from jax import lax
from jax.experimental import pallas as pl
from jax.experimental.pallas import tpu as pltpu
from jax.sharding import PartitionSpec as P

F32 = jnp.float32
BF16 = jnp.bfloat16
HALF = 24
NT = (((1,), (1,)), ((), ()))
VMEM = pl.BlockSpec(memory_space=pltpu.VMEM)
HBM = pl.BlockSpec(memory_space=pltpu.HBM)


def split(x):
    high = x.astype(BF16)
    return high, (x - high.astype(F32)).astype(BF16)


def banded(place_ref, offsets_ref, rows_of, blocks, window, total_blocks):
    block_cols, width, size, _ = blocks.shape
    first = place_ref[0]
    for c in range(block_cols):
        column = blocks[c].reshape(width * size, size)
        prod = lax.dot_general(rows_of(c), column, NT, preferred_element_type=F32)
        for k in range(width):
            row = jnp.clip(first + c + offsets_ref[k, c], 0, total_blocks - 1) - first + HALF
            window[row] += prod[:, size * k : size * (k + 1)]


def hand_out(place_ref, window, main, first_out, second_out):
    n = main.shape[0]
    main[...] = window[HALF : HALF + n]
    even = 1 - place_ref[2]
    first_out[...] = window[pl.ds(even * (HALF + n), HALF)].astype(BF16)
    second_out[...] = window[pl.ds((1 - even) * (HALF + n), HALF)].astype(BF16)


def shared(place_ref, b, n, first_in, second_in):
    odd = place_ref[2] == 1
    value = 0.0
    if b < HALF:
        value = value + jnp.where(odd, first_in[b], second_in[b]).astype(F32)
    if b >= n - HALF:
        edge = b - (n - HALF)
        value = value + jnp.where(odd, second_in[edge], first_in[edge]).astype(F32)
    return value


def fetch_kernel(place_ref, blocks_hbm, blocks, follows, sems):
    chunks = sems.shape[0]
    some = blocks.shape[0] // chunks
    copies = []
    for i in range(chunks):
        part = pl.ds(i * some, some)
        copies.append(pltpu.make_async_copy(blocks_hbm.at[part], blocks.at[part], sems.at[i]))
    for copy in copies:
        copy.start()
    follows[...] = jnp.where(place_ref[1] > 0, jnp.ones_like(follows), jnp.zeros_like(follows))
    for copy in copies:
        copy.wait()


def shells_kernel(
    total_blocks, place_ref, offsets_in, shells, older, blocks, follows,
    main, first_out, second_out, kept, window, offsets_ref, sem,
):
    fetched = pltpu.make_async_copy(offsets_in, offsets_ref, sem)
    fetched.start()
    window[...] = jnp.zeros_like(window)
    fetched.wait()
    banded(
        place_ref, offsets_ref,
        lambda c: jnp.concatenate([shells[c], older[c] * follows[...]], 0),
        blocks, window, total_blocks,
    )
    hand_out(place_ref, window, main, first_out, second_out)


def prepare_kernel(incident, element_map, inverse, source, inverse_parts):
    n, size, _ = inverse.shape
    samples = element_map.shape[1]
    unknown = lax.broadcasted_iota(jnp.int32, (size, samples), 0)
    line = lax.broadcasted_iota(jnp.int32, (8, samples), 0)
    for b in range(n):
        load = (unknown == element_map[b : b + 1, :]).astype(F32).astype(BF16)
        rows = jnp.zeros((8, samples), F32)
        for t in range(2):
            sample = jnp.broadcast_to(incident[t, b], (8, samples))
            high = sample.astype(BF16).astype(F32)
            rows = jnp.where(line == 2 * t, high, jnp.where(line == 2 * t + 1, sample - high, rows))
        out = lax.dot_general(rows.astype(BF16), load, NT, preferred_element_type=F32)
        for t in range(2):
            source[t, b : b + 1, :] = out[2 * t : 2 * t + 1] + out[2 * t + 1 : 2 * t + 2]
        high, low = split(inverse[b])
        inverse_parts[b, :, :size] = high
        inverse_parts[b, :, size:] = low


def combine_kernel(
    place_ref, main, first_in, second_in, source, keep, send1, send2, send3, total
):
    n, both, size = main.shape
    line = lax.broadcasted_iota(jnp.int32, (both, size), 0)
    for b in range(n):
        value = main[b] + shared(place_ref, b, n, first_in, second_in)
        for t in range(2):
            mine = line == place_ref[1] + t * (both // 2)
            value = value - jnp.where(mine, source[t, b : b + 1, :], 0.0)
        total[b] = value.astype(BF16)
    for distance, out in enumerate((keep, send1, send2, send3)):
        out[...] = total[quarter_of(place_ref, distance, n)]


def quarter_of(place_ref, distance, n):
    return pl.ds(((place_ref[1] & 3) ^ distance) * (n // 4), n // 4)


def gathered(place_ref, parts, rest):
    for distance, part in enumerate(parts):
        rest[quarter_of(place_ref, distance, rest.shape[0])] = part[...]


def solve(rest, inverse_part):
    pulses, size = rest.shape
    high, low = split(-rest)
    lhs = jnp.concatenate(
        [jnp.concatenate([high, high], 1), jnp.concatenate([low, jnp.zeros_like(low)], 1)], 0
    )
    out = lax.dot_general(lhs, inverse_part, NT, preferred_element_type=F32)
    return out[:pulses] + out[pulses:]


def first_step_kernel(
    total_blocks, place_ref, offsets_in, rest0, rest1, rest2, rest3, inverse_parts, blocks,
    current, main, first_out, second_out, rest, window, offsets_ref, sem,
):
    n, pulses, size = current.shape
    fetched = pltpu.make_async_copy(offsets_in, offsets_ref, sem)
    fetched.start()
    gathered(place_ref, (rest0, rest1, rest2, rest3), rest)
    for b in range(n):
        current[b] = solve(rest[b, :pulses].astype(F32), inverse_parts[b]).astype(BF16)
    fetched.wait()

    @pl.when(place_ref[1] == 0)
    def _():
        window[...] = jnp.zeros_like(window)
        banded(place_ref, offsets_ref, lambda c: current[c], blocks, window, total_blocks)
        hand_out(place_ref, window, main, first_out, second_out)


def second_sum_kernel(
    place_ref, rest0, rest1, rest2, rest3, main, current0, total, own_pulse, rest
):
    n, pulses, size = main.shape
    mine = lax.broadcasted_iota(jnp.int32, (pulses, size), 0) == place_ref[1]
    gathered(place_ref, (rest0, rest1, rest2, rest3), rest)
    for b in range(n):
        total[b] = rest[b, pulses:].astype(F32) + main[b]
        own = jnp.where(mine, current0[b].astype(F32), 0.0)
        own_pulse[b : b + 1, :] = jnp.sum(own, axis=0, keepdims=True)


def second_step_kernel(
    place_ref, total, first_in, second_in, inverse_parts, current, by_pulse, scratch
):
    n, pulses, size = current.shape

    @pl.when(place_ref[1] == 0)
    def _():
        for b in range(n):
            value = total[b] + shared(place_ref, b, n, first_in, second_in)
            new = solve(value, inverse_parts[b])
            current[b] = new.astype(BF16)
            scratch[b * pulses : (b + 1) * pulses, :] = new
        for p in range(pulses):
            by_pulse[p] = scratch[pl.ds(p, n, stride=pulses), :].astype(BF16)


def call(kernel, name, out_shape, in_specs, scratch_shapes=(), mib=16, aliases={}, cols=None):
    def placed(*refs):
        col = lax.axis_index("col")
        kernel((col * cols, lax.axis_index("lag"), lax.rem(col, 2)), *refs)

    return pl.pallas_call(
        kernel if cols is None else placed,
        name=name,
        out_shape=out_shape,
        in_specs=in_specs,
        out_specs=[VMEM] * len(out_shape),
        scratch_shapes=scratch_shapes,
        input_output_aliases=aliases,
        compiler_params=pltpu.CompilerParams(vmem_limit_bytes=mib * 2**20),
    )


def exchange(block, distance):
    return lax.ppermute(block, "lag", [(i, i ^ distance) for i in range(16)])


def added(own, others):
    return sum((other.astype(F32) for other in others), own.astype(F32)).astype(BF16)


def trade(first_out, second_out):
    n = lax.axis_size("col")
    pairs = [(i, i ^ 1) for i in range(n)]
    others = [(i, (i + 1 if i % 2 else i - 1) % n) for i in range(n)]
    second_in = lax.ppermute(second_out, "col", others)
    return lax.ppermute(first_out, "col", pairs), second_in


def body(blocks, offsets, history, instant_inverse, incident, element_map):
    lag_index = lax.axis_index("lag")
    lags = lax.axis_size("lag")
    n, pulses, size = history.shape[1:]
    total_blocks = n * lax.axis_size("col")
    blocks = blocks[0]
    band_rows = offsets[0].T
    shells = history[0]

    def shape(*dims, dtype=F32):
        return jax.ShapeDtypeStruct(dims, dtype)

    def partial_out(rows):
        edge = shape(HALF, rows, size, dtype=BF16)
        return shape(n, rows, size), edge, edge

    def window(rows):
        return pltpu.VMEM((n + 2 * HALF, rows, size), F32)

    kept = shape(*blocks.shape, dtype=BF16)
    offsets_here = [pltpu.SMEM(band_rows.shape, jnp.int32), pltpu.SemaphoreType.DMA]
    fetch = call(
        fetch_kernel, "fetch", (kept, shape(pulses, size, dtype=BF16)), [HBM], [pltpu.SemaphoreType.DMA((8,))], mib=40, cols=n
    )
    shell_sums = call(
        functools.partial(shells_kernel, total_blocks), "shell_sums",
        partial_out(2 * pulses) + (kept,), [VMEM] * 5, [window(2 * pulses)] + offsets_here,
        aliases={3: 3}, cols=n,
    )
    prepare = call(
        prepare_kernel, "prepare",
        (shape(2, n, size), shape(n, size, 2 * size, dtype=BF16)), [VMEM] * 3,
    )
    quarters = (shape(n // 4, 2 * pulses, size, dtype=BF16),) * 4
    rows = pltpu.VMEM((n, 2 * pulses, size), BF16)
    combine = call(combine_kernel, "combine", quarters, [VMEM] * 4, [rows], cols=n)
    first_step = call(
        functools.partial(first_step_kernel, total_blocks), "first_step",
        (shape(n, pulses, size, dtype=BF16),) + partial_out(pulses),
        [VMEM] * 7, [rows, window(pulses)] + offsets_here, cols=n,
    )
    second_sum = call(
        second_sum_kernel, "second_sum",
        (shape(n, pulses, size), shape(n, size)), [VMEM] * 6, [rows], cols=n,
    )
    second_step = call(
        second_step_kernel, "second_step",
        (shape(n, pulses, size, dtype=BF16), shape(pulses, n, size, dtype=BF16)),
        [VMEM] * 4, [pltpu.VMEM((n * pulses, size), F32)], cols=n,
    )

    older = lax.ppermute(shells, "lag", [(i, (i + 1) % lags) for i in range(lags)])
    with jax.named_scope("shells"):
        blocks, follows = fetch(blocks)
        main, first_out, second_out, blocks = shell_sums(
            band_rows, shells, older, blocks, follows
        )
    with jax.named_scope("halo"):
        first_in, second_in = trade(first_out, second_out)
    source, inverse_parts = prepare(incident, element_map, instant_inverse)
    keep, *sent = combine(main, first_in, second_in, source)
    with jax.named_scope("near"):
        quarter = added(keep, [exchange(sent[d - 1], d) for d in (3, 1, 2)])
    with jax.named_scope("far"):
        quarter = added(quarter, [exchange(quarter, d) for d in (8, 4, 12)])
    with jax.named_scope("gather"):
        by_distance = {d: exchange(quarter, d) for d in (3, 1, 2)}
        rest = [quarter] + [by_distance[d] for d in (1, 2, 3)]
    current0, extra, first_out, second_out = first_step(
        band_rows, *rest, inverse_parts, blocks
    )
    shells, current0 = lax.optimization_barrier((shells, current0))
    oldest = lax.ppermute(shells, "lag", [(i, (i + 2) % lags) for i in range(lags)])
    with jax.named_scope("halo_extra"):
        first_in, second_in = trade(first_out, second_out)
    total, own0 = second_sum(*rest, extra, current0)
    current1, by_pulse1 = second_step(total, first_in, second_in, inverse_parts)
    with jax.named_scope("spread"):
        quarter = pulses // 4
        groups = [by_pulse1[quarter * g : quarter * (g + 1)] for g in range(4)]
        arrived = [lax.ppermute(groups[g], "lag", [(0, 4 * g)]) for g in (1, 2, 3)]
        leader = groups[0]
        for g in (1, 2, 3):
            leader = jnp.where(lag_index == 4 * g, arrived[g - 1], leader)
        arrived = [
            lax.ppermute(leader[d], "lag", [(4 * g, 4 * g + d) for g in range(4)]) for d in (1, 2, 3)
        ]
        own1 = leader[0]
        for d in (1, 2, 3):
            own1 = jnp.where(lag_index % 4 == d, arrived[d - 1], own1)
    currents = jnp.stack([own0.astype(BF16), own1])[:, :, None, :]
    aged = jnp.where(lag_index == 0, current1, jnp.where(lag_index == 1, current0, oldest))
    return currents, aged[None]


def solution(mesh):
    placed = (
        P("lag", "col", None, None, None),
        P("lag", "col", None),
        P("lag", "col", None, None),
        P("col", None, None),
        P(None, "col", "lag", None),
        P("col", None),
    )
    return jax.shard_map(
        body,
        mesh=mesh,
        in_specs=placed,
        out_specs=(P(None, "col", "lag", None), P("lag", "col", None, None)),
        check_vma=False,
    )
```

```python
import functools

import jax
import jax.numpy as jnp
from jax import lax
from jax.experimental import pallas as pl
from jax.experimental.pallas import tpu as pltpu
from jax.sharding import PartitionSpec as P

F32 = jnp.float32
BF16 = jnp.bfloat16
HALF = 24
NT = (((1,), (1,)), ((), ()))
VMEM = pl.BlockSpec(memory_space=pltpu.VMEM)
HBM = pl.BlockSpec(memory_space=pltpu.HBM)


def split(x):
    high = x.astype(BF16)
    return high, (x - high.astype(F32)).astype(BF16)


def banded(place_ref, offsets_ref, rows_of, blocks, window, total_blocks):
    block_cols, width, size, _ = blocks.shape
    first = place_ref[0]
    for c in range(block_cols):
        column = blocks[c].reshape(width * size, size)
        prod = lax.dot_general(rows_of(c), column, NT, preferred_element_type=F32)
        for k in range(width):
            row = jnp.clip(first + c + offsets_ref[k, c], 0, total_blocks - 1) - first + HALF
            window[row] += prod[:, size * k : size * (k + 1)]


def hand_out(place_ref, window, main, first_out, second_out):
    n = main.shape[0]
    main[...] = window[HALF : HALF + n]
    even = 1 - place_ref[2]
    first_out[...] = window[pl.ds(even * (HALF + n), HALF)].astype(BF16)
    second_out[...] = window[pl.ds((1 - even) * (HALF + n), HALF)].astype(BF16)


def shared(place_ref, b, n, first_in, second_in):
    odd = place_ref[2] == 1
    value = 0.0
    if b < HALF:
        value = value + jnp.where(odd, first_in[b], second_in[b]).astype(F32)
    if b >= n - HALF:
        edge = b - (n - HALF)
        value = value + jnp.where(odd, second_in[edge], first_in[edge]).astype(F32)
    return value


def fetch_kernel(place_ref, blocks_hbm, blocks, follows, sems):
    chunks = sems.shape[0]
    some = blocks.shape[0] // chunks
    copies = []
    for i in range(chunks):
        part = pl.ds(i * some, some)
        copies.append(pltpu.make_async_copy(blocks_hbm.at[part], blocks.at[part], sems.at[i]))
    for copy in copies:
        copy.start()
    follows[...] = jnp.where(place_ref[1] > 0, jnp.ones_like(follows), jnp.zeros_like(follows))
    for copy in copies:
        copy.wait()


def shells_kernel(
    total_blocks, place_ref, offsets_in, shells, older, blocks, follows,
    main, first_out, second_out, kept, window, offsets_ref, sem,
):
    fetched = pltpu.make_async_copy(offsets_in, offsets_ref, sem)
    fetched.start()
    window[...] = jnp.zeros_like(window)
    fetched.wait()
    banded(
        place_ref, offsets_ref,
        lambda c: jnp.concatenate([shells[c], older[c] * follows[...]], 0),
        blocks, window, total_blocks,
    )
    hand_out(place_ref, window, main, first_out, second_out)


def prepare_kernel(incident, element_map, inverse, source, inverse_parts):
    n, size, _ = inverse.shape
    samples = element_map.shape[1]
    unknown = lax.broadcasted_iota(jnp.int32, (size, samples), 0)
    line = lax.broadcasted_iota(jnp.int32, (8, samples), 0)
    for b in range(n):
        load = (unknown == element_map[b : b + 1, :]).astype(F32).astype(BF16)
        rows = jnp.zeros((8, samples), F32)
        for t in range(2):
            sample = jnp.broadcast_to(incident[t, b], (8, samples))
            high = sample.astype(BF16).astype(F32)
            rows = jnp.where(line == 2 * t, high, jnp.where(line == 2 * t + 1, sample - high, rows))
        out = lax.dot_general(rows.astype(BF16), load, NT, preferred_element_type=F32)
        for t in range(2):
            source[t, b : b + 1, :] = out[2 * t : 2 * t + 1] + out[2 * t + 1 : 2 * t + 2]
        high, low = split(inverse[b])
        inverse_parts[b, :, :size] = high
        inverse_parts[b, :, size:] = low


def combine_kernel(
    place_ref, main, first_in, second_in, source, keep, send1, send2, send3, total
):
    n, both, size = main.shape
    line = lax.broadcasted_iota(jnp.int32, (both, size), 0)
    for b in range(n):
        value = main[b] + shared(place_ref, b, n, first_in, second_in)
        for t in range(2):
            mine = line == place_ref[1] + t * (both // 2)
            value = value - jnp.where(mine, source[t, b : b + 1, :], 0.0)
        total[b] = value.astype(BF16)
    for distance, out in enumerate((keep, send1, send2, send3)):
        out[...] = total[quarter_of(place_ref, distance, n)]


def quarter_of(place_ref, distance, n):
    return pl.ds(((place_ref[1] & 3) ^ distance) * (n // 4), n // 4)


def gathered(place_ref, parts, rest):
    for distance, part in enumerate(parts):
        rest[quarter_of(place_ref, distance, rest.shape[0])] = part[...]


def solve(rest, inverse_part):
    pulses, size = rest.shape
    high, low = split(-rest)
    lhs = jnp.concatenate(
        [jnp.concatenate([high, high], 1), jnp.concatenate([low, jnp.zeros_like(low)], 1)], 0
    )
    out = lax.dot_general(lhs, inverse_part, NT, preferred_element_type=F32)
    return out[:pulses] + out[pulses:]


def far_sum_kernel(place_ref, own, far1, far2, far3, inverse_parts, out):
    rows, both, size = own.shape
    pulses = both // 2
    inverse = inverse_parts.at[quarter_of(place_ref, 0, inverse_parts.shape[0])]
    for b in range(rows):
        total = sum(part[b].astype(F32) for part in (far1, far2, far3)) + own[b].astype(F32)
        out[b, :pulses] = solve(total[:pulses], inverse[b]).astype(BF16)
        out[b, pulses:] = total[pulses:].astype(BF16)


def first_step_kernel(
    total_blocks, place_ref, offsets_in, rest0, rest1, rest2, rest3, blocks,
    current, main, first_out, second_out, rest, window, offsets_ref, sem,
):
    n, pulses, size = current.shape
    fetched = pltpu.make_async_copy(offsets_in, offsets_ref, sem)
    fetched.start()
    gathered(place_ref, (rest0, rest1, rest2, rest3), rest)
    for b in range(n):
        current[b] = rest[b, :pulses]
    window[...] = jnp.zeros_like(window)
    fetched.wait()

    @pl.when(place_ref[1] == 0)
    def _():
        banded(place_ref, offsets_ref, lambda c: current[c], blocks, window, total_blocks)
        hand_out(place_ref, window, main, first_out, second_out)


def second_sum_kernel(
    place_ref, rest0, rest1, rest2, rest3, main, current0, total, own_pulse, rest
):
    n, pulses, size = main.shape
    mine = lax.broadcasted_iota(jnp.int32, (pulses, size), 0) == place_ref[1]
    gathered(place_ref, (rest0, rest1, rest2, rest3), rest)
    for b in range(n):
        total[b] = rest[b, pulses:].astype(F32) + main[b]
        own = jnp.where(mine, current0[b].astype(F32), 0.0)
        own_pulse[b : b + 1, :] = jnp.sum(own, axis=0, keepdims=True)


def second_step_kernel(
    place_ref, total, first_in, second_in, inverse_parts, current, by_pulse, scratch
):
    n, pulses, size = current.shape

    @pl.when(place_ref[1] == 0)
    def _():
        for b in range(n):
            value = total[b] + shared(place_ref, b, n, first_in, second_in)
            new = solve(value, inverse_parts[b])
            current[b] = new.astype(BF16)
            scratch[b * pulses : (b + 1) * pulses, :] = new
        for p in range(pulses):
            by_pulse[p] = scratch[pl.ds(p, n, stride=pulses), :].astype(BF16)


def call(kernel, name, out_shape, in_specs, scratch_shapes=(), mib=16, aliases={}, cols=None):
    def placed(*refs):
        col = lax.axis_index("col")
        kernel((col * cols, lax.axis_index("lag"), lax.rem(col, 2)), *refs)

    return pl.pallas_call(
        kernel if cols is None else placed,
        name=name,
        out_shape=out_shape,
        in_specs=in_specs,
        out_specs=[VMEM] * len(out_shape),
        scratch_shapes=scratch_shapes,
        input_output_aliases=aliases,
        compiler_params=pltpu.CompilerParams(vmem_limit_bytes=mib * 2**20),
    )


def exchange(block, distance):
    return lax.ppermute(block, "lag", [(i, i ^ distance) for i in range(16)])


def added(own, others):
    return sum((other.astype(F32) for other in others), own.astype(F32)).astype(BF16)


def trade(first_out, second_out):
    n = lax.axis_size("col")
    pairs = [(i, i ^ 1) for i in range(n)]
    others = [(i, (i + 1 if i % 2 else i - 1) % n) for i in range(n)]
    second_in = lax.ppermute(second_out, "col", others)
    return lax.ppermute(first_out, "col", pairs), second_in


def body(blocks, offsets, history, instant_inverse, incident, element_map):
    lag_index = lax.axis_index("lag")
    lags = lax.axis_size("lag")
    n, pulses, size = history.shape[1:]
    total_blocks = n * lax.axis_size("col")
    blocks = blocks[0]
    band_rows = offsets[0].T
    shells = history[0]

    def shape(*dims, dtype=F32):
        return jax.ShapeDtypeStruct(dims, dtype)

    def partial_out(rows):
        edge = shape(HALF, rows, size, dtype=BF16)
        return shape(n, rows, size), edge, edge

    def window(rows):
        return pltpu.VMEM((n + 2 * HALF, rows, size), F32)

    kept = shape(*blocks.shape, dtype=BF16)
    offsets_here = [pltpu.SMEM(band_rows.shape, jnp.int32), pltpu.SemaphoreType.DMA]
    fetch = call(
        fetch_kernel, "fetch", (kept, shape(pulses, size, dtype=BF16)), [HBM], [pltpu.SemaphoreType.DMA((8,))], mib=40, cols=n
    )
    shell_sums = call(
        functools.partial(shells_kernel, total_blocks), "shell_sums",
        partial_out(2 * pulses) + (kept,), [VMEM] * 5, [window(2 * pulses)] + offsets_here,
        aliases={3: 3}, cols=n,
    )
    prepare = call(
        prepare_kernel, "prepare",
        (shape(2, n, size), shape(n, size, 2 * size, dtype=BF16)), [VMEM] * 3,
    )
    quarters = (shape(n // 4, 2 * pulses, size, dtype=BF16),) * 4
    rows = pltpu.VMEM((n, 2 * pulses, size), BF16)
    combine = call(combine_kernel, "combine", quarters, [VMEM] * 4, [rows], cols=n)
    far_sum = call(far_sum_kernel, "far_sum", quarters[:1], [VMEM] * 5, cols=n)
    first_step = call(
        functools.partial(first_step_kernel, total_blocks), "first_step",
        (shape(n, pulses, size, dtype=BF16),) + partial_out(pulses),
        [VMEM] * 6, [rows, window(pulses)] + offsets_here, cols=n,
    )
    second_sum = call(
        second_sum_kernel, "second_sum",
        (shape(n, pulses, size), shape(n, size)), [VMEM] * 6, [rows], cols=n,
    )
    second_step = call(
        second_step_kernel, "second_step",
        (shape(n, pulses, size, dtype=BF16), shape(pulses, n, size, dtype=BF16)),
        [VMEM] * 4, [pltpu.VMEM((n * pulses, size), F32)], cols=n,
    )

    older = lax.ppermute(shells, "lag", [(i, (i + 1) % lags) for i in range(lags)])
    with jax.named_scope("shells"):
        blocks, follows = fetch(blocks)
        main, first_out, second_out, blocks = shell_sums(
            band_rows, shells, older, blocks, follows
        )
    with jax.named_scope("halo"):
        first_in, second_in = trade(first_out, second_out)
    source, inverse_parts = prepare(incident, element_map, instant_inverse)
    keep, *sent = combine(main, first_in, second_in, source)
    with jax.named_scope("near"):
        quarter = added(keep, [exchange(sent[d - 1], d) for d in (3, 1, 2)])
    with jax.named_scope("far"):
        far = [exchange(quarter, d) for d in (8, 4, 12)]
        (quarter,) = far_sum(quarter, *far, inverse_parts)
    with jax.named_scope("gather"):
        by_distance = {d: exchange(quarter, d) for d in (3, 1, 2)}
        rest = [quarter] + [by_distance[d] for d in (1, 2, 3)]
    current0, extra, first_out, second_out = first_step(
        band_rows, *rest, blocks
    )
    shells, current0 = lax.optimization_barrier((shells, current0))
    oldest = lax.ppermute(shells, "lag", [(i, (i + 2) % lags) for i in range(lags)])
    with jax.named_scope("halo_extra"):
        first_in, second_in = trade(first_out, second_out)
    total, own0 = second_sum(*rest, extra, current0)
    current1, by_pulse1 = second_step(total, first_in, second_in, inverse_parts)
    with jax.named_scope("spread"):
        quarter = pulses // 4
        groups = [by_pulse1[quarter * g : quarter * (g + 1)] for g in range(4)]
        arrived = [lax.ppermute(groups[g], "lag", [(0, 4 * g)]) for g in (1, 2, 3)]
        leader = groups[0]
        for g in (1, 2, 3):
            leader = jnp.where(lag_index == 4 * g, arrived[g - 1], leader)
        arrived = [
            lax.ppermute(leader[d], "lag", [(4 * g, 4 * g + d) for g in range(4)]) for d in (1, 2, 3)
        ]
        own1 = leader[0]
        for d in (1, 2, 3):
            own1 = jnp.where(lag_index % 4 == d, arrived[d - 1], own1)
    currents = jnp.stack([own0.astype(BF16), own1])[:, :, None, :]
    aged = jnp.where(lag_index == 0, current1, jnp.where(lag_index == 1, current0, oldest))
    return currents, aged[None]


def solution(mesh):
    placed = (
        P("lag", "col", None, None, None),
        P("lag", "col", None),
        P("lag", "col", None, None),
        P("col", None, None),
        P(None, "col", "lag", None),
        P("col", None),
    )
    return jax.shard_map(
        body,
        mesh=mesh,
        in_specs=placed,
        out_specs=(P(None, "col", "lag", None), P("lag", "col", None, None)),
        check_vma=False,
    )
```
